256 devices in a mesh: row: 16 (over z_lo, y), col: 16 (over x, z_hi, core).
Axes of the slice: x: 4, y: 4, z: 8 (z_hi: 2, z_lo: 4; z = z_hi * 4 + z_lo), core: 2. Of those that a mesh axis runs over, the one named last changes fastest.
Arguments:
- rhs: float32 [262144, 256], P(('row', 'col')), may hold values from -6 to 6
- local_mat: bfloat16 [262144, 1024], P(('row', 'col')), may hold values from -1 to 5
- local_inv: bfloat16 [262144, 1024], P(('row', 'col')), may hold values from -1 to 1
- basis_t: bfloat16 [24576, 1024], P(('row', 'col')), may hold values from -0.1875 to 0.1875
- coarse_inv: bfloat16 [24576, 24576], P('col', 'row'), may hold values from -0.0390625 to 0.0390625
- couple: float32 [256, 4, 128], P(('row', 'col')), may hold values from 0.5 to 2
- margin_rows: int32 [256, 4, 128], P(('row', 'col')), may hold values from 0 to 1023, as said below
Outputs:
- solution: float32 [262144, 256], P(('row', 'col'))
- residual: float32 [262144, 256], P(('row', 'col'))
The draws below stay inside these ranges and needn't reach their ends.
Inputs may be any that keep to these rules, and one draw needn't show every extreme that they name: `margin_rows`: within each subdomain the 512 listed rows are all different.
All inputs are finite; a program needn't handle non-finite values.
Results may differ from the reference program's by a relative error of at most 0.024.
Values may be sent and summed in bfloat16 or wider, within the bound.
A program may use at most 64 MiB of HBM per device.

```python
import math
import jax
import jax.numpy as jnp
from jax import lax

NLOC = 1024
CPD = 96
NRHS = 256
OVL = 128
STEPS = 2
SUBDOMAINS = 256
COARSE = 24576
N_ROW = 16
N_COL = 16


def dominant_blocks(key, low, high, spread):
    diagonal = jax.random.uniform(jax.random.fold_in(key, 11), (SUBDOMAINS, NLOC, 1), jnp.float32, low, high)
    spread_part = jax.random.normal(jax.random.fold_in(key, 13), (SUBDOMAINS, NLOC, NLOC), jnp.float32) * (spread / math.sqrt(NLOC))
    matrix = spread_part + diagonal * jnp.eye(NLOC, dtype=jnp.float32)
    return matrix.reshape(SUBDOMAINS * NLOC, NLOC).astype(jnp.bfloat16)


def draw_local_mat(key, part):
    return dominant_blocks(jax.random.fold_in(key, 21), 2.0, 4.0, 0.8)


def draw_local_inv(key, part):
    return dominant_blocks(jax.random.fold_in(key, 22), 0.25, 0.5, 0.12)


def draw_margin_rows(key, part):
    subkeys = jax.random.split(jax.random.fold_in(key, 23), SUBDOMAINS)
    orders = jax.vmap(lambda one_key: jax.random.permutation(one_key, NLOC))(subkeys)
    return orders[:, :4 * OVL].reshape(SUBDOMAINS, 4, OVL).astype(jnp.int32)


def block_scale(rng, shape, cuts, smallest, largest):
    loudness = 1.0
    for axis_at, blocks in cuts:
        heights = jax.random.uniform(jax.random.fold_in(jax.random.fold_in(rng, 6), axis_at), (blocks,), jnp.float32, smallest / len(cuts), largest / len(cuts))
        loudness = loudness * jnp.repeat(jnp.exp(heights), shape[axis_at] // blocks).reshape((-1,) + (1,) * (len(shape) - 1 - axis_at))
    return loudness


def bell_draw(own_key, dims, scale, most, pieces=(), held_as=jnp.bfloat16):
    entries = jax.random.normal(own_key, dims, jnp.float32) * scale
    if len(pieces) > 0:
        entries = block_scale(own_key, dims, pieces, -0.22, 0.18) * entries
    return jnp.clip(entries, min=-most, max=most).astype(held_as)


def setup_inputs(seed: int = 0) -> dict:
    key_of = jax.random.split(jax.random.key(seed), 8)
    rhs = bell_draw(key_of[0], (SUBDOMAINS * NLOC, NRHS), 1.0, 6.0, ((0, 256),), jnp.float32)
    local_mat = draw_local_mat(jax.random.fold_in(key_of[7], 71), 0)
    local_inv = draw_local_inv(jax.random.fold_in(key_of[7], 71), 0)
    basis_t = bell_draw(key_of[3], (COARSE, NLOC), NLOC ** -0.5, 0.1875, ((0, 256),))
    coarse_inv = bell_draw(key_of[4], (COARSE, COARSE), COARSE ** -0.5, 0.0390625, ((0, 16), (1, 16)))
    couple = jnp.clip(0.5 + 1.5 * jax.random.uniform(key_of[5], (SUBDOMAINS, 4, OVL), jnp.float32) ** block_scale(key_of[5], (SUBDOMAINS, 4, OVL), ((0, 256),), -0.2, 0.2), 0.5, 2.0)
    margin_rows = draw_margin_rows(jax.random.fold_in(key_of[7], 71), 0)
    return dict(rhs=rhs, local_mat=local_mat, local_inv=local_inv, basis_t=basis_t, coarse_inv=coarse_inv, couple=couple, margin_rows=margin_rows)


def apply_operator(vector, local_mat, couple, margin_rows):
    vector_b = vector.astype(jnp.bfloat16).reshape(SUBDOMAINS, NLOC, NRHS)
    face_vals = jax.vmap(lambda block, rows_of: block[rows_of])(vector_b, margin_rows)
    face_grid = face_vals.reshape(N_ROW, N_COL, 4, OVL, NRHS)
    padded = jnp.pad(face_grid, ((1, 1), (1, 1), (0, 0), (0, 0), (0, 0)))
    from_north = padded[:-2, 1:-1, 1]
    from_south = padded[2:, 1:-1, 0]
    from_west = padded[1:-1, :-2, 3]
    from_east = padded[1:-1, 2:, 2]
    received = jnp.stack([from_north, from_south, from_west, from_east], axis=2)
    received = received.reshape(SUBDOMAINS, 4, OVL, NRHS).astype(jnp.float32)
    coupling_terms = couple[:, :, :, None] * received

    def scatter_one(rows_of, values):
        return jnp.zeros((NLOC, NRHS), jnp.float32).at[rows_of.reshape(-1)].add(values.reshape(-1, NRHS))

    coupled = jax.vmap(scatter_one)(margin_rows, coupling_terms)
    matrices = local_mat.reshape(SUBDOMAINS, NLOC, NLOC)
    product = lax.map(lambda pair: jnp.dot(pair[0], pair[1], preferred_element_type=jnp.float32), (matrices, vector_b))
    return (product - coupled).reshape(SUBDOMAINS * NLOC, NRHS)


def coarse_correction(residual, basis_t, coarse_inv):
    rounded = residual.astype(jnp.bfloat16).reshape(SUBDOMAINS, NLOC, NRHS)
    basis = basis_t.reshape(SUBDOMAINS, CPD, NLOC)
    restricted = lax.map(lambda pair: jnp.dot(pair[0], pair[1], preferred_element_type=jnp.float32), (basis, rounded))
    restricted = restricted.astype(jnp.bfloat16).reshape(COARSE, NRHS)
    permuted = jnp.dot(coarse_inv, restricted, preferred_element_type=jnp.float32)
    coarse_part = permuted.reshape(N_COL, N_ROW, CPD, NRHS).transpose(1, 0, 2, 3).reshape(SUBDOMAINS, CPD, NRHS)
    coarse_b = coarse_part.astype(jnp.bfloat16)
    correction = lax.map(lambda pair: jnp.dot(pair[0].T, pair[1], preferred_element_type=jnp.float32), (basis, coarse_b))
    return correction.reshape(SUBDOMAINS * NLOC, NRHS)


def local_solve(residual, local_inv):
    rounded = residual.astype(jnp.bfloat16).reshape(SUBDOMAINS, NLOC, NRHS)
    inverses = local_inv.reshape(SUBDOMAINS, NLOC, NLOC)
    solved = lax.map(lambda pair: jnp.dot(pair[0], pair[1], preferred_element_type=jnp.float32), (inverses, rounded))
    return solved.reshape(SUBDOMAINS * NLOC, NRHS)


def reference(rhs, local_mat, local_inv, basis_t, coarse_inv, couple, margin_rows):
    solution = jnp.zeros(rhs.shape, jnp.float32)
    residual = rhs
    for sweep in range(STEPS):
        if sweep > 0:
            residual = rhs - apply_operator(solution, local_mat, couple, margin_rows)
        solution = solution + coarse_correction(residual, basis_t, coarse_inv)
        residual = rhs - apply_operator(solution, local_mat, couple, margin_rows)
        solution = solution + local_solve(residual, local_inv)
    residual = rhs - apply_operator(solution, local_mat, couple, margin_rows)
    return solution, residual
```

```python
import jax
import jax.numpy as jnp
from jax import lax
from jax.experimental import pallas as pl
from jax.experimental.pallas import tpu as pltpu
from jax.sharding import PartitionSpec as P

STEPS = 2
NLOC = 1024
CPD = 96
NRHS = 256
OVL = 128
COARSE_BLOCK = 1536
GROUP = 384
FACES = 4 * OVL
MESH = pl.DeviceIdType.MESH
F32 = jnp.float32
BF16 = jnp.bfloat16


def dot(a, b):
    return jnp.dot(a, b, preferred_element_type=F32)


def dot_lhs_t(a, b):
    return lax.dot_general(a, b, (((0,), (0,)), ((), ())), preferred_element_type=F32)


def rows(start, size):
    return pl.ds(pl.multiple_of(start, 32), size)


def kernel(
    rhs_h, lmat_h, linv_h, basis_h, cinv_h, couple_h, margin_h,
    sol_out, res_out,
    rhs, lmat, linv, basis, cinv, couple, margin,
    sol, base, base_b, vb, face, face_b, recv,
    gath, acc, part, ybuf, qbuf, zbuf,
    st, wrow, bs, sbt, bt, lsw, sl, slsw, pre, pre_face, coarse_b,
    ag_s, ag_r, rs_s, rs_r, h_s, h_r, ld, out_sem,
):
    r = lax.axis_index("row")
    c = lax.axis_index("col")
    zl, y = r // 4, r % 4
    x, zh, k = c // 4, (c // 2) % 2, c % 2

    loads = [
        pltpu.make_async_copy(s, d, ld.at[i])
        for i, (s, d) in enumerate(
            (
                (rhs_h, rhs), (basis_h, basis), (couple_h, couple), (margin_h, margin),
                (linv_h, linv), (cinv_h, cinv), (lmat_h, lmat),
            )
        )
    ]
    for cp in loads:
        cp.start()

    sibling = (r, x * 4 + zh * 2 + (1 - k))
    z_partner = (r, x * 4 + (1 - zh) * 2 + k)
    shifts = (2, 1, 3)
    x_to = [(r, ((x + d) % 4) * 4 + zh * 2 + k) for d in shifts]
    x_from = [(x + 4 - d) % 4 for d in shifts]
    y_to = [(zl * 4 + (y + d) % 4, c) for d in shifts]
    z_to = [((zl + d) % 4 * 4 + y, c) for d in shifts]
    halo = (
        (r > 0, (r - 1, c), 1),
        (r < 15, (r + 1, c), 0),
        (c > 0, (r, c - 1), 3),
        (c < 15, (r, c + 1), 2),
    )

    for f, (there, _, _2) in enumerate(halo):
        @pl.when(jnp.logical_not(there))
        def _():
            for h in range(2 * STEPS):
                recv[h, pl.ds(f * OVL, OVL), :] = jnp.zeros((OVL, NRHS), BF16)

    barrier = pltpu.get_barrier_semaphore()
    others = [sibling, z_partner] + x_to + y_to + z_to
    for dev in others:
        pl.semaphore_signal(barrier, inc=1, device_id=dev, device_id_type=MESH)
    count = len(others)
    for there, dev, _ in halo:
        @pl.when(there)
        def _():
            pl.semaphore_signal(barrier, inc=1, device_id=dev, device_id_type=MESH)
        count = count + jnp.where(there, 1, 0)

    sends = []

    def send(src, dst, ssem, rsem, dev):
        cp = pltpu.make_async_remote_copy(
            src_ref=src, dst_ref=dst, send_sem=ssem, recv_sem=rsem,
            device_id=dev, device_id_type=MESH,
        )
        cp.start()
        sends.append(cp)
        return cp

    def halo_copy(h, f):
        there, dev, slot = halo[f]
        return pltpu.make_async_remote_copy(
            src_ref=face_b.at[h, pl.ds(f * OVL, OVL)],
            dst_ref=recv.at[h, pl.ds(slot * OVL, OVL)],
            send_sem=h_s.at[h, f], recv_sem=h_r.at[h, slot],
            device_id=dev, device_id_type=MESH,
        )

    def arriving_copy(h, f):
        _, dev, _2 = halo[f]
        return pltpu.make_async_remote_copy(
            src_ref=face_b.at[h, pl.ds(f * OVL, OVL)],
            dst_ref=recv.at[h, pl.ds(f * OVL, OVL)],
            send_sem=h_s.at[h, f], recv_sem=h_r.at[h, f],
            device_id=dev, device_id_type=MESH,
        )

    def halo_start(h):
        for f in (2, 3, 0, 1):
            @pl.when(halo[f][0])
            def _():
                halo_copy(h, f).start()

    def halo_wait(h):
        for f in range(4):
            @pl.when(halo[f][0])
            def _():
                arriving_copy(h, f).wait_recv()

    def halo_sent():
        for h in range(2 * STEPS):
            for f in range(4):
                @pl.when(halo[f][0])
                def _():
                    halo_copy(h, f).wait_send()

    def block(ref, at):
        return ref.at[rows(at * CPD, CPD)]

    def coarse(s, between):
        g = gath.at[s]
        copies = {}

        def go(n, at, dev):
            copies[n] = send(block(g, at), block(g, at), ag_s.at[s, n], ag_r.at[s, n], dev)

        go(0, c, z_partner)
        for j in range(3):
            go(1 + j, c, x_to[j])
        go(4, c, sibling)
        between()
        for j in (1, 2, 0):
            copies[1 + j].wait_recv()
            go(5 + j, x_from[j] * 4 + zh * 2 + k, sibling)
        copies[0].wait_recv()
        zs = x * 4 + (1 - zh) * 2 + k
        for j in range(3):
            go(8 + j, zs, x_to[j])
        go(11, zs, sibling)

        def chunk(xg, first):
            cols = pl.ds(pl.multiple_of(xg * GROUP, 128), GROUP)
            right = g[rows(xg * GROUP, GROUP), :]

            @pl.loop(0, 4)
            def _(m):
                at = rows(m * GROUP, GROUP)
                p = dot(cinv[at, cols], right)
                if first:
                    acc[at, :] = p
                else:
                    acc[at, :] += p

        copies[4].wait_recv()
        copies[11].wait_recv()
        chunk(x, True)
        for j in (1, 2, 0):
            copies[8 + j].wait_recv()
            go(12 + j, x_from[j] * 4 + (1 - zh) * 2 + k, sibling)
        for j in (1, 2):
            copies[5 + j].wait_recv()
            copies[12 + j].wait_recv()
            chunk(x_from[j], False)
        copies[5].wait_recv()
        copies[12].wait_recv()

        p_ref = part.at[s]
        cols = pl.ds(pl.multiple_of(x_from[0] * GROUP, 128), GROUP)
        right = g[rows(x_from[0] * GROUP, GROUP), :]
        ycopies = {}
        for a, dz in enumerate((2, 1, 3, 0)):
            t = (zl + dz) % 4
            at = rows(t * GROUP, GROUP)
            total = acc[at, :] + dot(cinv[at, cols], right)
            acc[at, :] = total
            p_ref[at, :] = total.astype(BF16)
            for j, d in enumerate(shifts):
                n = a * 3 + j
                ycopies[a, j] = send(
                    block(p_ref, t * 4 + (y + d) % 4), ybuf.at[s, n],
                    rs_s.at[s, n], rs_r.at[s, n], y_to[j],
                )
        zcopies = []

        def over_y(a, t):
            for j in range(3):
                ycopies[a, j].wait_recv()
            total = acc[rows((t * 4 + y) * CPD, CPD), :]
            for j in range(3):
                total = total + ybuf[s, a * 3 + j].astype(F32)
            return total

        for a, dz in enumerate((2, 1, 3)):
            t = (zl + dz) % 4
            qbuf[s, a] = over_y(a, t).astype(BF16)
            zcopies.append(
                send(qbuf.at[s, a], zbuf.at[s, a], rs_s.at[s, 12 + a], rs_r.at[s, 12 + a], z_to[a])
            )
        total = over_y(3, zl)
        for a in range(3):
            zcopies[a].wait_recv()
            total = total + zbuf[s, a].astype(F32)
        coarse_b[...] = total.astype(BF16)

    def prepare():
        for i in (2, 3, 4):
            loads[i].wait()
        w = [couple[0, f : f + 1, :] for f in range(4)]

        @pl.loop(0, 8)
        def _(m):
            at = rows(m * 128, 128)
            ids = lax.broadcasted_iota(jnp.int32, (128, OVL), 0) + m * 128
            total = jnp.zeros((128, OVL), F32)
            for f in range(4):
                hit = ids == margin[0, f : f + 1, :]
                st[at, pl.ds(f * OVL, OVL)] = jnp.where(hit, 1.0, 0.0).astype(BF16)
                total = total + jnp.where(hit, w[f], 0.0)
            wrow[at, :] = jnp.broadcast_to(jnp.sum(total, axis=1, keepdims=True), (128, OVL))

        wide = jnp.concatenate(w, axis=1)
        picked = dot(basis[...], st[...])
        bs[...] = (picked * wide).astype(BF16)
        sbt[...] = picked.T.astype(BF16)
        bt[...] = basis[...].astype(F32).T.astype(BF16)

        @pl.loop(0, 4)
        def _(m):
            at = rows(m * 256, 256)
            lsw[at, :] = (dot(linv[at, :], st[...]) * wide).astype(BF16)

        for m in range(4):
            pick = st[:, m * OVL : (m + 1) * OVL].astype(F32).T.astype(BF16)
            at = pl.ds(m * OVL, OVL)
            sl[at, :] = dot(pick, linv[...]).astype(BF16)
            slsw[at, :] = dot(pick, lsw[...]).astype(BF16)
        loads[5].wait()

    def tiles(fn, size=256, total=NLOC):
        @pl.loop(0, total // size)
        def _(m):
            fn(rows(m * size, size))

    loads[0].wait()
    loads[1].wait()
    base_b[...] = rhs[...].astype(BF16)
    gath[0, rows(c * CPD, CPD), :] = dot(basis[...], base_b[...]).astype(BF16)
    pl.semaphore_wait(barrier, count)

    for s in range(STEPS):
        h = 2 * s
        coarse(s, prepare if s == 0 else lambda: None)

        moved = dot(sbt[...], coarse_b[...])
        if s > 0:
            moved = moved + face[...]
        face[...] = moved
        face_b[h] = moved.astype(BF16)
        halo_start(h)

        def correct(at):
            v = dot(bt[at, :], coarse_b[...])
            if s > 0:
                v = v + sol[at, :]
            sol[at, :] = v
            vb[at, :] = v.astype(BF16)

        tiles(correct)
        if s == 0:
            loads[6].wait()

        def defect(at):
            base_b[at, :] = (rhs[at, :] - dot(lmat[at, :], vb[...])).astype(BF16)

        tiles(defect)

        def face_pre(at):
            pre_face[at, :] = face[at, :] + dot(sl[at, :], base_b[...])

        tiles(face_pre, 256, FACES)

        def solve_pre(at):
            sol[at, :] += dot(linv[at, :], base_b[...])

        tiles(solve_pre)
        halo_wait(h)

        moved = pre_face[...] + dot(slsw[...], recv[h])
        face[...] = moved
        face_b[h + 1] = moved.astype(BF16)
        halo_start(h + 1)

        def solve(at):
            v = sol[at, :] + dot(lsw[at, :], recv[h])
            sol[at, :] = v
            vb[at, :] = v.astype(BF16)

        tiles(solve)
        last = s == STEPS - 1
        if last:
            written = pltpu.make_async_copy(sol, sol_out, out_sem.at[0])
            written.start()

        def defect2(at):
            v = rhs[at, :] - dot(lmat[at, :], vb[...])
            if last:
                base[at, :] = v
            else:
                base_b[at, :] = v.astype(BF16)

        tiles(defect2)
        if not last:
            pre[...] = dot(basis[...], base_b[...])
            halo_wait(h + 1)
            gath[s + 1, rows(c * CPD, CPD), :] = (pre[...] + dot(bs[...], recv[h + 1])).astype(BF16)
        else:
            halo_wait(h + 1)

            def finish(at):
                w = jnp.concatenate([wrow[at, :]] * 2, axis=1)
                base[at, :] += w * dot(st[at, :], recv[h + 1])

            tiles(finish)
            residual = pltpu.make_async_copy(base, res_out, out_sem.at[1])
            residual.start()
            written.wait()
            residual.wait()

    for cp in sends:
        cp.wait_send()
    halo_sent()


def per_device(*args):
    any_space = pl.BlockSpec(memory_space=pl.ANY)
    vm = pltpu.VMEM
    dma = pltpu.SemaphoreType.DMA
    scratch = [vm(a.shape, a.dtype) for a in args] + [
        vm((NLOC, NRHS), F32),
        vm((NLOC, NRHS), F32),
        vm((NLOC, NRHS), BF16),
        vm((NLOC, NRHS), BF16),
        vm((FACES, NRHS), F32),
        vm((2 * STEPS, FACES, NRHS), BF16),
        vm((2 * STEPS, FACES, NRHS), BF16),
        vm((STEPS, COARSE_BLOCK, NRHS), BF16),
        vm((COARSE_BLOCK, NRHS), F32),
        vm((STEPS, COARSE_BLOCK, NRHS), BF16),
        vm((STEPS, 12, CPD, NRHS), BF16),
        vm((STEPS, 3, CPD, NRHS), BF16),
        vm((STEPS, 3, CPD, NRHS), BF16),
        vm((NLOC, FACES), BF16),
        vm((NLOC, OVL), F32),
        vm((CPD, FACES), BF16),
        vm((FACES, CPD), BF16),
        vm((NLOC, CPD), BF16),
        vm((NLOC, FACES), BF16),
        vm((FACES, NLOC), BF16),
        vm((FACES, FACES), BF16),
        vm((CPD, NRHS), F32),
        vm((FACES, NRHS), F32),
        vm((CPD, NRHS), BF16),
        dma((STEPS, 15)), dma((STEPS, 15)),
        dma((STEPS, 15)), dma((STEPS, 15)),
        dma((2 * STEPS, 4)), dma((2 * STEPS, 4)),
        dma((len(args),)), dma((2,)),
    ]
    out = jax.ShapeDtypeStruct((NLOC, NRHS), F32)
    return pl.pallas_call(
        kernel,
        out_shape=(out, out),
        in_specs=[any_space] * len(args),
        out_specs=(any_space, any_space),
        scratch_shapes=scratch,
        name="schwarz",
        compiler_params=pltpu.CompilerParams(
            collective_id=0, has_side_effects=True, vmem_limit_bytes=48 << 20
        ),
    )(*args)


def solution(mesh):
    whole = P(("row", "col"), None)
    stacked = P(("row", "col"), None, None)
    return jax.shard_map(
        per_device,
        mesh=mesh,
        in_specs=(whole, whole, whole, whole, P("col", "row"), stacked, stacked),
        out_specs=(whole, whole),
        check_vma=False,
    )
```

```python
import jax
import jax.numpy as jnp
from jax import lax
from jax.experimental import pallas as pl
from jax.experimental.pallas import tpu as pltpu
from jax.sharding import PartitionSpec as P

STEPS = 2
NLOC = 1024
CPD = 96
NRHS = 256
OVL = 128
COARSE_BLOCK = 1536
GROUP = 384
FACES = 4 * OVL
PARTS = 2
WIDTH = NRHS // PARTS
MESH = pl.DeviceIdType.MESH
F32 = jnp.float32
BF16 = jnp.bfloat16


def dot(a, b):
    return jnp.dot(a, b, preferred_element_type=F32)


def dot_lhs_t(a, b):
    return lax.dot_general(a, b, (((0,), (0,)), ((), ())), preferred_element_type=F32)


def rows(start, size):
    return pl.ds(pl.multiple_of(start, 32), size)


def kernel(
    rhs_h, lmat_h, linv_h, basis_h, cinv_h, couple_h, margin_h,
    sol_out, base_out, recv_out, st_out, wrow_out,
    rhs, lmat, linv, basis, cinv, couple, margin,
    sol, base, base_b, vb, face, face_b, recv,
    gath, acc, part, ybuf, qbuf, zbuf,
    st, wrow, bs, sbt, bt, lsw, sl, slsw, pre, pre_face, coarse_b,
    ag_s, ag_r, rs_s, rs_r, h_s, h_r, ld, out_sem,
):
    r = lax.axis_index("row")
    c = lax.axis_index("col")
    zl, y = r // 4, r % 4
    x, zh, k = c // 4, (c // 2) % 2, c % 2

    loads = [
        pltpu.make_async_copy(s, d, ld.at[i])
        for i, (s, d) in enumerate(
            (
                (rhs_h, rhs), (basis_h, basis), (couple_h, couple), (margin_h, margin),
                (linv_h, linv), (cinv_h, cinv), (lmat_h, lmat),
            )
        )
    ]
    for cp in loads[:4]:
        cp.start()

    sibling = (r, x * 4 + zh * 2 + (1 - k))
    z_partner = (r, x * 4 + (1 - zh) * 2 + k)
    shifts = (2, 1, 3)
    x_to = [(r, ((x + d) % 4) * 4 + zh * 2 + k) for d in shifts]
    x_from = [(x + 4 - d) % 4 for d in shifts]
    y_to = [(zl * 4 + (y + d) % 4, c) for d in shifts]
    z_other = [3 - 3 * (zl // 2), 2 - zl // 2, zl + 1 - 2 * (zl % 2)]
    z_to = [(t * 4 + y, c) for t in z_other]
    halo = (
        (r > 0, (r - 1, c), 1),
        (r < 15, (r + 1, c), 0),
        (c > 0, (r, c - 1), 3),
        (c < 15, (r, c + 1), 2),
    )

    for f, (there, _, _2) in enumerate(halo):
        @pl.when(jnp.logical_not(there))
        def _():
            for h in range(2 * STEPS):
                for p in range(PARTS):
                    recv[h, p, pl.ds(f * OVL, OVL), :] = jnp.zeros((OVL, WIDTH), BF16)

    barrier = pltpu.get_barrier_semaphore()
    others = [sibling, z_partner] + x_to + y_to + z_to
    for dev in others:
        pl.semaphore_signal(barrier, inc=1, device_id=dev, device_id_type=MESH)
    count = len(others)
    for there, dev, _ in halo:
        @pl.when(there)
        def _():
            pl.semaphore_signal(barrier, inc=1, device_id=dev, device_id_type=MESH)
        count = count + jnp.where(there, 1, 0)

    sends = []

    def send(src, dst, ssem, rsem, dev):
        cp = pltpu.make_async_remote_copy(
            src_ref=src, dst_ref=dst, send_sem=ssem, recv_sem=rsem,
            device_id=dev, device_id_type=MESH,
        )
        cp.start()
        sends.append(cp)
        return cp

    def lanes(p):
        return pl.ds(p * WIDTH, WIDTH)

    def halo_copy(h, p, f, slot):
        return pltpu.make_async_remote_copy(
            src_ref=face_b.at[h, p, pl.ds(f * OVL, OVL)],
            dst_ref=recv.at[h, p, pl.ds(slot * OVL, OVL)],
            send_sem=h_s.at[h, p, f], recv_sem=h_r.at[h, p, slot],
            device_id=halo[f][1], device_id_type=MESH,
        )

    def halo_start(h, p):
        for f in (2, 3, 0, 1):
            @pl.when(halo[f][0])
            def _():
                halo_copy(h, p, f, halo[f][2]).start()

    def halo_wait(h, p):
        for f in (1, 0, 3, 2):
            @pl.when(halo[f][0])
            def _():
                halo_copy(h, p, f, f).wait_recv()

    def halo_sent():
        for h in range(2 * STEPS):
            for p in range(PARTS):
                for f in range(4):
                    @pl.when(halo[f][0])
                    def _():
                        halo_copy(h, p, f, halo[f][2]).wait_send()

    def block(ref, at):
        return ref.at[rows(at * CPD, CPD)]

    copies = {}
    own = [xg * 4 + zh * 2 + k for xg in x_from]
    other = [xg * 4 + (1 - zh) * 2 + k for xg in x_from]
    across = x * 4 + (1 - zh) * 2 + k

    def go(s, p, n, at, dev):
        g = gath.at[s, p]
        copies[p, n] = send(block(g, at), block(g, at), ag_s.at[s, p, n], ag_r.at[s, p, n], dev)

    def gather_start(s, p):
        go(s, p, 0, c, z_partner)
        for j in range(3):
            go(s, p, 1 + j, c, x_to[j])
        go(s, p, 4, c, sibling)

    def chunk(s, p, xg, first):
        cols = pl.ds(pl.multiple_of(xg * GROUP, 128), GROUP)
        right = gath[s, p, rows(xg * GROUP, GROUP), :]
        for m in range(4):
            at = pl.ds(m * GROUP, GROUP)
            v = dot(cinv[at, cols], right)
            if first:
                acc[p, at, :] = v
            else:
                acc[p, at, :] += v

    def coarse(s, before, after):
        before()
        for p in range(PARTS):
            for j in (1, 2, 0):
                copies[p, 1 + j].wait_recv()
                go(s, p, 5 + j, own[j], sibling)
        for p in range(PARTS):
            copies[p, 0].wait_recv()
            for j in range(3):
                go(s, p, 8 + j, across, x_to[j])
            go(s, p, 11, across, sibling)
        for p in range(PARTS):
            copies[p, 4].wait_recv()
            copies[p, 11].wait_recv()
            chunk(s, p, x, True)
        for p in range(PARTS):
            for j in (1, 2, 0):
                copies[p, 8 + j].wait_recv()
                go(s, p, 12 + j, other[j], sibling)
        ycopies = {}
        for p in range(PARTS):
            for j in (1, 2):
                copies[p, 5 + j].wait_recv()
                copies[p, 12 + j].wait_recv()
                chunk(s, p, x_from[j], False)
            copies[p, 5].wait_recv()
            copies[p, 12].wait_recv()

            p_ref = part.at[s, p]
            cols = pl.ds(pl.multiple_of(x_from[0] * GROUP, 128), GROUP)
            right = gath[s, p, rows(x_from[0] * GROUP, GROUP), :]
            for a, t in enumerate(z_other + [zl]):
                at = rows(t * GROUP, GROUP)
                total = acc[p, at, :] + dot(cinv[at, cols], right)
                acc[p, at, :] = total
                p_ref[at, :] = total.astype(BF16)
                for j, d in enumerate(shifts):
                    n = a * 3 + j
                    ycopies[p, a, j] = send(
                        block(p_ref, t * 4 + (y + d) % 4), ybuf.at[s, p, n],
                        rs_s.at[s, p, n], rs_r.at[s, p, n], y_to[j],
                    )
        after()

        def over_y(p, a, t):
            for j in range(3):
                ycopies[p, a, j].wait_recv()
            total = acc[p, rows((t * 4 + y) * CPD, CPD), :]
            for j in range(3):
                total = total + ybuf[s, p, a * 3 + j].astype(F32)
            return total

        for p in range(PARTS):
            for a, t in enumerate(z_other):
                qbuf[s, p, a] = over_y(p, a, t).astype(BF16)
                send(
                    qbuf.at[s, p, a], zbuf.at[s, p, zl],
                    rs_s.at[s, p, 12 + a], rs_r.at[s, p, 12 + zl], z_to[a],
                )
        for p in range(PARTS):
            total = over_y(p, 3, zl)
            for a, t in reversed(list(enumerate(z_other))):
                pltpu.make_async_remote_copy(
                    src_ref=qbuf.at[s, p, a], dst_ref=zbuf.at[s, p, t],
                    send_sem=rs_s.at[s, p, 12 + a], recv_sem=rs_r.at[s, p, 12 + t],
                    device_id=z_to[a], device_id_type=MESH,
                ).wait_recv()
                total = total + zbuf[s, p, t].astype(F32)
            coarse_b[:, lanes(p)] = total.astype(BF16)
            moved = dot(sbt[...], coarse_b[:, lanes(p)])
            if s > 0:
                moved = moved + face[:, lanes(p)]
            face[:, lanes(p)] = moved
            face_b[2 * s, p] = moved.astype(BF16)
            halo_start(2 * s, p)

    def prepare_faces():
        for i in (2, 3):
            loads[i].wait()
        w = [couple[0, f : f + 1, :] for f in range(4)]
        for m in range(4):
            at = pl.ds(m * 256, 256)
            ids = lax.broadcasted_iota(jnp.int32, (256, OVL), 0) + m * 256
            total = jnp.zeros((256, OVL), F32)
            for f in range(4):
                hit = ids == margin[0, f : f + 1, :]
                st[at, pl.ds(f * OVL, OVL)] = jnp.where(hit, 1.0, 0.0).astype(BF16)
                total = total + jnp.where(hit, w[f], 0.0)
            wrow[at, :] = jnp.broadcast_to(jnp.sum(total, axis=1, keepdims=True), (256, OVL))
        keep(4, st, st_out)
        keep(5, wrow, wrow_out)
        loads[5].wait()

    def prepare_local():
        loads[4].wait()
        wide = jnp.concatenate([couple[0, f : f + 1, :] for f in range(4)], axis=1)
        picked = dot(basis[...], st[...])
        bs[...] = (picked * wide).astype(BF16)
        sbt[...] = picked.T.astype(BF16)
        bt[...] = basis[...].astype(F32).T.astype(BF16)
        for m in range(4):
            at = pl.ds(m * 256, 256)
            lsw[at, :] = (dot(linv[at, :], st[...]) * wide).astype(BF16)
        for m in range(4):
            pick = st[:, m * OVL : (m + 1) * OVL].astype(F32).T.astype(BF16)
            at = pl.ds(m * OVL, OVL)
            sl[at, :] = dot(pick, linv[...]).astype(BF16)
            slsw[at, :] = dot(pick, lsw[...]).astype(BF16)

    def tiles(fn, size=256, total=NLOC):
        for m in range(total // size):
            fn(pl.ds(m * size, size))

    kept = []

    def keep(n, src, dst):
        cp = pltpu.make_async_copy(src, dst, out_sem.at[n])
        cp.start()
        kept.append(cp)

    loads[0].wait()
    base_b[...] = rhs[...].astype(BF16)
    loads[1].wait()
    first = dot(basis[...], base_b[...]).astype(BF16)
    for p in range(PARTS):
        gath[0, p, rows(c * CPD, CPD), :] = first[:, p * WIDTH : (p + 1) * WIDTH]
    for cp in loads[4:]:
        cp.start()
    pl.semaphore_wait(barrier, count)
    for p in range(PARTS):
        gather_start(0, p)

    for s in range(STEPS):
        h = 2 * s
        last = s == STEPS - 1
        coarse(s, *((prepare_faces, prepare_local) if s == 0 else (lambda: None,) * 2))

        def correct(at):
            v = dot(bt[at, :], coarse_b[...])
            if s > 0:
                v = v + sol[at, :]
            sol[at, :] = v
            vb[at, :] = v.astype(BF16)

        tiles(correct)
        if s == 0:
            loads[6].wait()

        def defect(at):
            base_b[at, :] = (rhs[at, :] - dot(lmat[at, :], vb[...])).astype(BF16)

        tiles(defect)

        def face_pre(at):
            pre_face[at, :] = face[at, :] + dot(sl[at, :], base_b[...])

        tiles(face_pre, 256, FACES)

        for p in range(PARTS):
            halo_wait(h, p)
            moved = pre_face[:, lanes(p)] + dot(slsw[...], recv[h, p])
            face[:, lanes(p)] = moved
            face_b[h + 1, p] = moved.astype(BF16)
            halo_start(h + 1, p)

        def solve(at):
            v = sol[at, :] + dot(linv[at, :], base_b[...])
            for p in range(PARTS):
                w = v[:, p * WIDTH : (p + 1) * WIDTH] + dot(lsw[at, :], recv[h, p])
                sol[at, lanes(p)] = w
                vb[at, lanes(p)] = w.astype(BF16)

        tiles(solve)
        if last:
            keep(0, sol, sol_out)

        def defect2(at):
            v = rhs[at, :] - dot(lmat[at, :], vb[...])
            if last:
                base[at, :] = v
            else:
                base_b[at, :] = v.astype(BF16)

        tiles(defect2)
        if not last:
            pre[...] = dot(basis[...], base_b[...])
            for p in range(PARTS):
                halo_wait(h + 1, p)
                gath[s + 1, p, rows(c * CPD, CPD), :] = (
                    pre[:, lanes(p)] + dot(bs[...], recv[h + 1, p])
                ).astype(BF16)
                gather_start(s + 1, p)
        else:
            keep(1, base, base_out)
            for p in range(PARTS):
                halo_wait(h + 1, p)
                keep(2 + p, recv.at[h + 1, p], recv_out.at[p])

    for cp in kept:
        cp.wait()
    for cp in sends:
        cp.wait_send()
    halo_sent()


def last_residual(sol, base, recv, st, wrow, sol_out, res_out, res, sem):
    copies = [pltpu.make_async_copy(sol, sol_out, sem.at[4])]
    copies[0].start()
    right = jnp.concatenate([recv[p] for p in range(PARTS)], axis=1)
    for m in range(4):
        at = pl.ds(m * 256, 256)
        w = jnp.concatenate([wrow[at, :]] * PARTS, axis=1)
        res[at, :] = base[at, :] + w * dot(st[at, :], right)
        cp = pltpu.make_async_copy(res.at[at], res_out.at[at], sem.at[m])
        cp.start()
        copies.append(cp)
    for cp in copies:
        cp.wait()


def per_device(*args):
    args = [pltpu.with_memory_space_constraint(a, pltpu.HBM) for a in args]
    any_space = pl.BlockSpec(memory_space=pl.ANY)
    vm = pltpu.VMEM
    dma = pltpu.SemaphoreType.DMA
    scratch = [vm(a.shape, a.dtype) for a in args] + [
        vm((NLOC, NRHS), F32),
        vm((NLOC, NRHS), F32),
        vm((NLOC, NRHS), BF16),
        vm((NLOC, NRHS), BF16),
        vm((FACES, NRHS), F32),
        vm((2 * STEPS, PARTS, FACES, WIDTH), BF16),
        vm((2 * STEPS, PARTS, FACES, WIDTH), BF16),
        vm((STEPS, PARTS, COARSE_BLOCK, WIDTH), BF16),
        vm((PARTS, COARSE_BLOCK, WIDTH), F32),
        vm((STEPS, PARTS, COARSE_BLOCK, WIDTH), BF16),
        vm((STEPS, PARTS, 12, CPD, WIDTH), BF16),
        vm((STEPS, PARTS, 3, CPD, WIDTH), BF16),
        vm((STEPS, PARTS, 4, CPD, WIDTH), BF16),
        vm((NLOC, FACES), BF16),
        vm((NLOC, OVL), F32),
        vm((CPD, FACES), BF16),
        vm((FACES, CPD), BF16),
        vm((NLOC, CPD), BF16),
        vm((NLOC, FACES), BF16),
        vm((FACES, NLOC), BF16),
        vm((FACES, FACES), BF16),
        vm((CPD, NRHS), F32),
        vm((FACES, NRHS), F32),
        vm((CPD, NRHS), BF16),
        dma((STEPS, PARTS, 15)), dma((STEPS, PARTS, 15)),
        dma((STEPS, PARTS, 15)), dma((STEPS, PARTS, 16)),
        dma((2 * STEPS, PARTS, 4)), dma((2 * STEPS, PARTS, 4)),
        dma((len(args),)), dma((6,)),
    ]
    out = jax.ShapeDtypeStruct((NLOC, NRHS), F32)
    handed_on = (
        out,
        out,
        jax.ShapeDtypeStruct((PARTS, FACES, WIDTH), BF16),
        jax.ShapeDtypeStruct((NLOC, FACES), BF16),
        jax.ShapeDtypeStruct((NLOC, OVL), F32),
    )
    handed = pl.pallas_call(
        kernel,
        out_shape=handed_on,
        in_specs=[any_space] * len(args),
        out_specs=(any_space,) * 5,
        scratch_shapes=scratch,
        name="schwarz",
        compiler_params=pltpu.CompilerParams(
            collective_id=0, has_side_effects=True, vmem_limit_bytes=48 << 20
        ),
    )(*args)
    return pl.pallas_call(
        last_residual,
        out_shape=(out, out),
        in_specs=[any_space] + [pl.BlockSpec(memory_space=vm)] * 4,
        out_specs=(pl.BlockSpec(memory_space=pltpu.HBM), pl.BlockSpec(memory_space=pltpu.HBM)),
        scratch_shapes=[vm((NLOC, NRHS), F32), dma((5,))],
        name="last_residual",
        compiler_params=pltpu.CompilerParams(vmem_limit_bytes=24 << 20),
    )(*handed)


def solution(mesh):
    whole = P(("row", "col"), None)
    stacked = P(("row", "col"), None, None)
    return jax.shard_map(
        per_device,
        mesh=mesh,
        in_specs=(whole, whole, whole, whole, P("col", "row"), stacked, stacked),
        out_specs=(whole, whole),
        check_vma=False,
    )
```

```python
import jax
import jax.numpy as jnp
from jax import lax
from jax.experimental import pallas as pl
from jax.experimental.pallas import tpu as pltpu
from jax.sharding import PartitionSpec as P

STEPS = 2
NLOC = 1024
CPD = 96
NRHS = 256
OVL = 128
COARSE_BLOCK = 1536
GROUP = 384
FACES = 4 * OVL
PARTS = 2
WIDTH = NRHS // PARTS
MESH = pl.DeviceIdType.MESH
F32 = jnp.float32
BF16 = jnp.bfloat16


def dot(a, b):
    return jnp.dot(a, b, preferred_element_type=F32)


def dot_lhs_t(a, b):
    return lax.dot_general(a, b, (((0,), (0,)), ((), ())), preferred_element_type=F32)


def rows(start, size):
    return pl.ds(pl.multiple_of(start, 32), size)


def kernel(
    rhs_h, lmat_h, linv_h, basis_h, cinv_h, couple_h, margin_h,
    sol_out, base_out, recv_out, st_out, wrow_out,
    rhs, lmat, linv, basis, cinv, couple, margin,
    sol, base, base_b, vb, face, face_b, recv,
    gath, acc, part, ybuf, qbuf, zbuf,
    st, wrow, bs, sbt, bt, lsw, sl, slsw, pre, pre_face, coarse_b,
    ag_s, ag_r, rs_s, rs_r, h_s, h_r, ld, out_sem,
):
    r = lax.axis_index("row")
    c = lax.axis_index("col")
    zl, y = r // 4, r % 4
    x, zh, k = c // 4, (c // 2) % 2, c % 2

    loads = [
        pltpu.make_async_copy(s, d, ld.at[i])
        for i, (s, d) in enumerate(
            (
                (rhs_h, rhs), (basis_h, basis), (couple_h, couple), (margin_h, margin),
                (linv_h, linv), (cinv_h, cinv), (lmat_h, lmat),
            )
        )
    ]
    for cp in loads[:4]:
        cp.start()

    sibling = (r, x * 4 + zh * 2 + (1 - k))
    z_partner = (r, x * 4 + (1 - zh) * 2 + k)
    shifts = (2, 1, 3)
    x_to = [(r, ((x + d) % 4) * 4 + zh * 2 + k) for d in shifts]
    x_from = [(x + 4 - d) % 4 for d in shifts]
    y_to = [(zl * 4 + (y + d) % 4, c) for d in shifts]
    z_other = [3 - 3 * (zl // 2), 2 - zl // 2, zl + 1 - 2 * (zl % 2)]
    z_to = [(t * 4 + y, c) for t in z_other]
    halo = (
        (r > 0, (r - 1, c), 1),
        (r < 15, (r + 1, c), 0),
        (c > 0, (r, c - 1), 3),
        (c < 15, (r, c + 1), 2),
    )

    for f, (there, _, _2) in enumerate(halo):
        @pl.when(jnp.logical_not(there))
        def _():
            for h in range(2 * STEPS):
                for p in range(PARTS):
                    recv[h, p, pl.ds(f * OVL, OVL), :] = jnp.zeros((OVL, WIDTH), BF16)

    barrier = pltpu.get_barrier_semaphore()
    others = [sibling, z_partner] + x_to + y_to + z_to
    for dev in others:
        pl.semaphore_signal(barrier, inc=1, device_id=dev, device_id_type=MESH)
    count = len(others)
    for there, dev, _ in halo:
        @pl.when(there)
        def _():
            pl.semaphore_signal(barrier, inc=1, device_id=dev, device_id_type=MESH)
        count = count + jnp.where(there, 1, 0)

    sends = []

    def send(src, dst, ssem, rsem, dev):
        cp = pltpu.make_async_remote_copy(
            src_ref=src, dst_ref=dst, send_sem=ssem, recv_sem=rsem,
            device_id=dev, device_id_type=MESH,
        )
        cp.start()
        sends.append(cp)
        return cp

    def lanes(p):
        return pl.ds(p * WIDTH, WIDTH)

    def halo_copy(h, p, f, slot):
        return pltpu.make_async_remote_copy(
            src_ref=face_b.at[h, p, pl.ds(f * OVL, OVL)],
            dst_ref=recv.at[h, p, pl.ds(slot * OVL, OVL)],
            send_sem=h_s.at[h, p, f], recv_sem=h_r.at[h, p, slot],
            device_id=halo[f][1], device_id_type=MESH,
        )

    def halo_start(h, p):
        for f in (2, 3, 0, 1):
            @pl.when(halo[f][0])
            def _():
                halo_copy(h, p, f, halo[f][2]).start()

    def halo_wait(h, p):
        for f in (1, 0, 3, 2):
            @pl.when(halo[f][0])
            def _():
                halo_copy(h, p, f, f).wait_recv()

    def halo_sent():
        for h in range(2 * STEPS):
            for p in range(PARTS):
                for f in range(4):
                    @pl.when(halo[f][0])
                    def _():
                        halo_copy(h, p, f, halo[f][2]).wait_send()

    def block(ref, at):
        return ref.at[rows(at * CPD, CPD)]

    copies = {}
    own = [xg * 4 + zh * 2 + k for xg in x_from]
    other = [xg * 4 + (1 - zh) * 2 + k for xg in x_from]
    across = x * 4 + (1 - zh) * 2 + k

    def go(s, p, n, at, dev):
        g = gath.at[s, p]
        copies[p, n] = send(block(g, at), block(g, at), ag_s.at[s, p, n], ag_r.at[s, p, n], dev)

    def gather_z(s, p):
        go(s, p, 0, c, z_partner)

    def gather_rest(s, p):
        for j in range(3):
            go(s, p, 1 + j, c, x_to[j])
        go(s, p, 4, c, sibling)

    def chunk(s, p, xg, first):
        cols = pl.ds(pl.multiple_of(xg * GROUP, 128), GROUP)
        right = gath[s, p, rows(xg * GROUP, GROUP), :]
        for m in range(4):
            at = pl.ds(m * GROUP, GROUP)
            v = dot(cinv[at, cols], right)
            if first:
                acc[p, at, :] = v
            else:
                acc[p, at, :] += v

    def coarse(s, before, after):
        before()
        for p in range(PARTS):
            for j in (1, 2, 0):
                copies[p, 1 + j].wait_recv()
                go(s, p, 5 + j, own[j], sibling)
        for p in range(PARTS):
            copies[p, 0].wait_recv()
            for j in range(3):
                go(s, p, 8 + j, across, x_to[j])
            go(s, p, 11, across, sibling)
        for p in range(PARTS):
            copies[p, 4].wait_recv()
            copies[p, 11].wait_recv()
            chunk(s, p, x, True)
        def pass_on(p, j):
            copies[p, 8 + j].wait_recv()
            go(s, p, 12 + j, other[j], sibling)

        def early(p, j):
            copies[p, 5 + j].wait_recv()
            copies[p, 12 + j].wait_recv()
            chunk(s, p, x_from[j], False)

        for p in range(PARTS):
            for j in (1, 2):
                pass_on(p, j)
        pass_on(0, 0)
        early(0, 1)
        pass_on(1, 0)
        early(0, 2)
        ycopies = {}

        def over_links(p, a, t):
            p_ref = part.at[s, p]
            for j, d in enumerate(shifts):
                n = a * 3 + j
                ycopies[p, a, j] = send(
                    block(p_ref, t * 4 + (y + d) % 4), ybuf.at[s, p, n],
                    rs_s.at[s, p, n], rs_r.at[s, p, n], y_to[j],
                )

        for p in range(PARTS):
            if p > 0:
                early(p, 1)
                early(p, 2)
            copies[p, 5].wait_recv()
            copies[p, 12].wait_recv()

            p_ref = part.at[s, p]
            cols = pl.ds(pl.multiple_of(x_from[0] * GROUP, 128), GROUP)
            right = gath[s, p, rows(x_from[0] * GROUP, GROUP), :]
            for a, t in enumerate(z_other + [zl]):
                at = rows(t * GROUP, GROUP)
                total = acc[p, at, :] + dot(cinv[at, cols], right)
                acc[p, at, :] = total
                p_ref[at, :] = total.astype(BF16)
                if a < 3:
                    over_links(p, a, t)
        for p in range(PARTS):
            over_links(p, 3, zl)
        after()

        def over_y(p, a, t):
            for j in range(3):
                ycopies[p, a, j].wait_recv()
            total = acc[p, rows((t * 4 + y) * CPD, CPD), :]
            for j in range(3):
                total = total + ybuf[s, p, a * 3 + j].astype(F32)
            return total

        for p in range(PARTS):
            for a, t in enumerate(z_other):
                qbuf[s, p, a] = over_y(p, a, t).astype(BF16)
                send(
                    qbuf.at[s, p, a], zbuf.at[s, p, zl],
                    rs_s.at[s, p, 12 + a], rs_r.at[s, p, 12 + zl], z_to[a],
                )
        for p in range(PARTS):
            total = over_y(p, 3, zl)
            for a, t in reversed(list(enumerate(z_other))):
                pltpu.make_async_remote_copy(
                    src_ref=qbuf.at[s, p, a], dst_ref=zbuf.at[s, p, t],
                    send_sem=rs_s.at[s, p, 12 + a], recv_sem=rs_r.at[s, p, 12 + t],
                    device_id=z_to[a], device_id_type=MESH,
                ).wait_recv()
                total = total + zbuf[s, p, t].astype(F32)
            coarse_b[:, lanes(p)] = total.astype(BF16)
            moved = dot(sbt[...], coarse_b[:, lanes(p)])
            if s > 0:
                moved = moved + face[:, lanes(p)]
            face[:, lanes(p)] = moved
            face_b[2 * s, p] = moved.astype(BF16)
            halo_start(2 * s, p)

    def prepare_faces():
        for i in (2, 3):
            loads[i].wait()
        w = [couple[0, f : f + 1, :] for f in range(4)]
        for m in range(4):
            at = pl.ds(m * 256, 256)
            ids = lax.broadcasted_iota(jnp.int32, (256, OVL), 0) + m * 256
            total = jnp.zeros((256, OVL), F32)
            for f in range(4):
                hit = ids == margin[0, f : f + 1, :]
                st[at, pl.ds(f * OVL, OVL)] = jnp.where(hit, 1.0, 0.0).astype(BF16)
                total = total + jnp.where(hit, w[f], 0.0)
            wrow[at, :] = jnp.broadcast_to(jnp.sum(total, axis=1, keepdims=True), (256, OVL))
        keep(4, st, st_out)
        keep(5, wrow, wrow_out)
        loads[5].wait()

    def prepare_local():
        loads[4].wait()
        wide = jnp.concatenate([couple[0, f : f + 1, :] for f in range(4)], axis=1)
        picked = dot(basis[...], st[...])
        bs[...] = (picked * wide).astype(BF16)
        sbt[...] = picked.T.astype(BF16)
        bt[...] = basis[...].astype(F32).T.astype(BF16)
        for m in range(4):
            at = pl.ds(m * 256, 256)
            lsw[at, :] = (dot(linv[at, :], st[...]) * wide).astype(BF16)
        for m in range(4):
            pick = st[:, m * OVL : (m + 1) * OVL].astype(F32).T.astype(BF16)
            at = pl.ds(m * OVL, OVL)
            sl[at, :] = dot(pick, linv[...]).astype(BF16)
            slsw[at, :] = dot(pick, lsw[...]).astype(BF16)

    def tiles(fn, size=256, total=NLOC):
        for m in range(total // size):
            fn(pl.ds(m * size, size))

    kept = []

    def keep(n, src, dst):
        cp = pltpu.make_async_copy(src, dst, out_sem.at[n])
        cp.start()
        kept.append(cp)

    loads[0].wait()
    base_b[...] = rhs[...].astype(BF16)
    loads[1].wait()
    first = dot(basis[...], base_b[...]).astype(BF16)
    for p in range(PARTS):
        gath[0, p, rows(c * CPD, CPD), :] = first[:, p * WIDTH : (p + 1) * WIDTH]
    for cp in loads[4:]:
        cp.start()
    pl.semaphore_wait(barrier, count)
    for p in range(PARTS):
        gather_z(0, p)
    for p in range(PARTS):
        gather_rest(0, p)

    for s in range(STEPS):
        h = 2 * s
        last = s == STEPS - 1
        coarse(s, *((prepare_faces, prepare_local) if s == 0 else (lambda: None,) * 2))

        def correct(at):
            v = dot(bt[at, :], coarse_b[...])
            if s > 0:
                v = v + sol[at, :]
            sol[at, :] = v
            vb[at, :] = v.astype(BF16)

        tiles(correct)
        if s == 0:
            loads[6].wait()

        def defect(at):
            base_b[at, :] = (rhs[at, :] - dot(lmat[at, :], vb[...])).astype(BF16)

        tiles(defect)

        def face_pre(at):
            pre_face[at, :] = face[at, :] + dot(sl[at, :], base_b[...])

        tiles(face_pre, 256, FACES)

        for p in range(PARTS):
            halo_wait(h, p)
            moved = pre_face[:, lanes(p)] + dot(slsw[...], recv[h, p])
            face[:, lanes(p)] = moved
            face_b[h + 1, p] = moved.astype(BF16)
            halo_start(h + 1, p)

        def solve(at):
            v = sol[at, :] + dot(linv[at, :], base_b[...])
            for p in range(PARTS):
                w = v[:, p * WIDTH : (p + 1) * WIDTH] + dot(lsw[at, :], recv[h, p])
                sol[at, lanes(p)] = w
                vb[at, lanes(p)] = w.astype(BF16)

        tiles(solve)
        if last:
            keep(0, sol, sol_out)

        def defect2(at):
            v = rhs[at, :] - dot(lmat[at, :], vb[...])
            if last:
                base[at, :] = v
            else:
                base_b[at, :] = v.astype(BF16)

        tiles(defect2)
        if not last:
            pre[...] = dot(basis[...], base_b[...])
            for p in range(PARTS):
                halo_wait(h + 1, p)
                gath[s + 1, p, rows(c * CPD, CPD), :] = (
                    pre[:, lanes(p)] + dot(bs[...], recv[h + 1, p])
                ).astype(BF16)
                gather_z(s + 1, p)
                gather_rest(s + 1, p)
        else:
            keep(1, base, base_out)
            for p in range(PARTS):
                halo_wait(h + 1, p)
                keep(2 + p, recv.at[h + 1, p], recv_out.at[p])

    for cp in kept:
        cp.wait()
    for cp in sends:
        cp.wait_send()
    halo_sent()


def last_residual(sol, base, recv, st, wrow, sol_out, res_out, res, sem):
    copies = [pltpu.make_async_copy(sol, sol_out, sem.at[4])]
    copies[0].start()
    right = jnp.concatenate([recv[p] for p in range(PARTS)], axis=1)
    for m in range(4):
        at = pl.ds(m * 256, 256)
        w = jnp.concatenate([wrow[at, :]] * PARTS, axis=1)
        res[at, :] = base[at, :] + w * dot(st[at, :], right)
        cp = pltpu.make_async_copy(res.at[at], res_out.at[at], sem.at[m])
        cp.start()
        copies.append(cp)
    for cp in copies:
        cp.wait()


def per_device(*args):
    args = [pltpu.with_memory_space_constraint(a, pltpu.HBM) for a in args]
    any_space = pl.BlockSpec(memory_space=pl.ANY)
    vm = pltpu.VMEM
    dma = pltpu.SemaphoreType.DMA
    scratch = [vm(a.shape, a.dtype) for a in args] + [
        vm((NLOC, NRHS), F32),
        vm((NLOC, NRHS), F32),
        vm((NLOC, NRHS), BF16),
        vm((NLOC, NRHS), BF16),
        vm((FACES, NRHS), F32),
        vm((2 * STEPS, PARTS, FACES, WIDTH), BF16),
        vm((2 * STEPS, PARTS, FACES, WIDTH), BF16),
        vm((STEPS, PARTS, COARSE_BLOCK, WIDTH), BF16),
        vm((PARTS, COARSE_BLOCK, WIDTH), F32),
        vm((STEPS, PARTS, COARSE_BLOCK, WIDTH), BF16),
        vm((STEPS, PARTS, 12, CPD, WIDTH), BF16),
        vm((STEPS, PARTS, 3, CPD, WIDTH), BF16),
        vm((STEPS, PARTS, 4, CPD, WIDTH), BF16),
        vm((NLOC, FACES), BF16),
        vm((NLOC, OVL), F32),
        vm((CPD, FACES), BF16),
        vm((FACES, CPD), BF16),
        vm((NLOC, CPD), BF16),
        vm((NLOC, FACES), BF16),
        vm((FACES, NLOC), BF16),
        vm((FACES, FACES), BF16),
        vm((CPD, NRHS), F32),
        vm((FACES, NRHS), F32),
        vm((CPD, NRHS), BF16),
        dma((STEPS, PARTS, 15)), dma((STEPS, PARTS, 15)),
        dma((STEPS, PARTS, 15)), dma((STEPS, PARTS, 16)),
        dma((2 * STEPS, PARTS, 4)), dma((2 * STEPS, PARTS, 4)),
        dma((len(args),)), dma((6,)),
    ]
    out = jax.ShapeDtypeStruct((NLOC, NRHS), F32)
    handed_on = (
        out,
        out,
        jax.ShapeDtypeStruct((PARTS, FACES, WIDTH), BF16),
        jax.ShapeDtypeStruct((NLOC, FACES), BF16),
        jax.ShapeDtypeStruct((NLOC, OVL), F32),
    )
    handed = pl.pallas_call(
        kernel,
        out_shape=handed_on,
        in_specs=[any_space] * len(args),
        out_specs=(any_space,) * 5,
        scratch_shapes=scratch,
        name="schwarz",
        compiler_params=pltpu.CompilerParams(
            collective_id=0, has_side_effects=True, vmem_limit_bytes=48 << 20
        ),
    )(*args)
    return pl.pallas_call(
        last_residual,
        out_shape=(out, out),
        in_specs=[any_space] + [pl.BlockSpec(memory_space=vm)] * 4,
        out_specs=(pl.BlockSpec(memory_space=pltpu.HBM), pl.BlockSpec(memory_space=pltpu.HBM)),
        scratch_shapes=[vm((NLOC, NRHS), F32), dma((5,))],
        name="last_residual",
        compiler_params=pltpu.CompilerParams(vmem_limit_bytes=24 << 20),
    )(*handed)


def solution(mesh):
    whole = P(("row", "col"), None)
    stacked = P(("row", "col"), None, None)
    return jax.shard_map(
        per_device,
        mesh=mesh,
        in_specs=(whole, whole, whole, whole, P("col", "row"), stacked, stacked),
        out_specs=(whole, whole),
        check_vma=False,
    )
```

```python
import jax
import jax.numpy as jnp
from jax import lax
from jax.experimental import pallas as pl
from jax.experimental.pallas import tpu as pltpu
from jax.sharding import PartitionSpec as P

STEPS = 2
NLOC = 1024
CPD = 96
NRHS = 256
OVL = 128
COARSE_BLOCK = 1536
GROUP = 384
FACES = 4 * OVL
PARTS = 2
WIDTH = NRHS // PARTS
MESH = pl.DeviceIdType.MESH
F32 = jnp.float32
BF16 = jnp.bfloat16


def dot(a, b):
    return jnp.dot(a, b, preferred_element_type=F32)


def dot_lhs_t(a, b):
    return lax.dot_general(a, b, (((0,), (0,)), ((), ())), preferred_element_type=F32)


def rows(start, size):
    return pl.ds(pl.multiple_of(start, 32), size)


def kernel(
    rhs_h, lmat_h, linv_h, basis_h, cinv_h, couple_h, margin_h,
    sol_out, base_out, recv_out, st_out, wrow_out,
    rhs, lmat, linv, basis, cinv, couple, margin,
    sol, base, base_b, vb, face, face_b, recv,
    gath, acc, part, ybuf, qbuf, zbuf, xbuf, xsum, xin,
    st, wrow, bs, sbt, bt, lsw, sl, slsw, pre, pre_face, coarse_b,
    ag_s, ag_r, rs_s, rs_r, h_s, h_r, ld, out_sem,
):
    r = lax.axis_index("row")
    c = lax.axis_index("col")
    zl, y = r // 4, r % 4
    x, zh, k = c // 4, (c // 2) % 2, c % 2

    loads = [
        pltpu.make_async_copy(s, d, ld.at[i])
        for i, (s, d) in enumerate(
            (
                (rhs_h, rhs), (basis_h, basis), (couple_h, couple), (margin_h, margin),
                (linv_h, linv), (cinv_h, cinv), (lmat_h, lmat),
            )
        )
    ]
    for cp in loads[:4]:
        cp.start()

    sibling = (r, x * 4 + zh * 2 + (1 - k))
    z_partner = (r, x * 4 + (1 - zh) * 2 + k)
    shifts = (2, 1, 3)
    x_to = [(r, ((x + d) % 4) * 4 + zh * 2 + k) for d in shifts]
    x_from = [(x + 4 - d) % 4 for d in shifts]
    y_to = [(zl * 4 + (y + d) % 4, c) for d in shifts]
    z_other = [3 - 3 * (zl // 2), 2 - zl // 2, zl + 1 - 2 * (zl % 2)]
    z_to = [(t * 4 + y, c) for t in z_other]
    halo = (
        (r > 0, (r - 1, c), 1),
        (r < 15, (r + 1, c), 0),
        (c > 0, (r, c - 1), 3),
        (c < 15, (r, c + 1), 2),
    )

    for f, (there, _, _2) in enumerate(halo):
        @pl.when(jnp.logical_not(there))
        def _():
            for h in range(2 * STEPS):
                for p in range(PARTS):
                    recv[h, p, pl.ds(f * OVL, OVL), :] = jnp.zeros((OVL, WIDTH), BF16)

    barrier = pltpu.get_barrier_semaphore()
    others = [sibling, z_partner] + x_to + y_to + z_to
    for dev in others:
        pl.semaphore_signal(barrier, inc=1, device_id=dev, device_id_type=MESH)
    count = len(others)
    for there, dev, _ in halo:
        @pl.when(there)
        def _():
            pl.semaphore_signal(barrier, inc=1, device_id=dev, device_id_type=MESH)
        count = count + jnp.where(there, 1, 0)

    sends = []

    def send(src, dst, ssem, rsem, dev):
        cp = pltpu.make_async_remote_copy(
            src_ref=src, dst_ref=dst, send_sem=ssem, recv_sem=rsem,
            device_id=dev, device_id_type=MESH,
        )
        cp.start()
        sends.append(cp)
        return cp

    def lanes(p):
        return pl.ds(p * WIDTH, WIDTH)

    def halo_copy(h, p, f, slot):
        return pltpu.make_async_remote_copy(
            src_ref=face_b.at[h, p, pl.ds(f * OVL, OVL)],
            dst_ref=recv.at[h, p, pl.ds(slot * OVL, OVL)],
            send_sem=h_s.at[h, p, f], recv_sem=h_r.at[h, p, slot],
            device_id=halo[f][1], device_id_type=MESH,
        )

    def halo_start(h, p):
        for f in (2, 3, 0, 1):
            @pl.when(halo[f][0])
            def _():
                halo_copy(h, p, f, halo[f][2]).start()

    def halo_wait(h, p):
        for f in (1, 0, 3, 2):
            @pl.when(halo[f][0])
            def _():
                halo_copy(h, p, f, f).wait_recv()

    def halo_sent():
        for h in range(2 * STEPS):
            for p in range(PARTS):
                for f in range(4):
                    @pl.when(halo[f][0])
                    def _():
                        halo_copy(h, p, f, halo[f][2]).wait_send()

    def block(ref, at):
        return ref.at[rows(at * CPD, CPD)]

    copies = {}
    own = [xg * 4 + zh * 2 + k for xg in x_from]
    other = [xg * 4 + (1 - zh) * 2 + k for xg in x_from]
    across = x * 4 + (1 - zh) * 2 + k

    def go(s, p, n, at, dev):
        g = gath.at[s, p]
        copies[p, n] = send(block(g, at), block(g, at), ag_s.at[s, p, n], ag_r.at[s, p, n], dev)

    def gather_z(s, p):
        go(s, p, 0, c, z_partner)

    def gather_rest(s, p):
        for j in range(3):
            go(s, p, 1 + j, c, x_to[j])
        go(s, p, 4, c, sibling)

    def chunk(s, p, xg, first):
        cols = pl.ds(pl.multiple_of(xg * GROUP, 128), GROUP)
        right = gath[s, p, rows(xg * GROUP, GROUP), :]
        for m in range(4):
            at = pl.ds(m * GROUP, GROUP)
            v = dot(cinv[at, cols], right)
            if first:
                acc[p, at, :] = v
            else:
                acc[p, at, :] += v

    def coarse(s, before, after):
        before()
        for p in range(PARTS):
            for j in (1, 2, 0):
                copies[p, 1 + j].wait_recv()
                go(s, p, 5 + j, own[j], sibling)
        for p in range(PARTS):
            copies[p, 0].wait_recv()
            for j in range(3):
                go(s, p, 8 + j, across, x_to[j])
            go(s, p, 11, across, sibling)
        for p in range(PARTS):
            copies[p, 4].wait_recv()
            copies[p, 11].wait_recv()
            chunk(s, p, x, True)
        def pass_on(p, j):
            copies[p, 8 + j].wait_recv()
            go(s, p, 12 + j, other[j], sibling)

        def early(p, j):
            copies[p, 5 + j].wait_recv()
            copies[p, 12 + j].wait_recv()
            chunk(s, p, x_from[j], False)

        for p in range(PARTS):
            for j in (1, 2):
                pass_on(p, j)
        pass_on(0, 0)
        early(0, 1)
        pass_on(1, 0)
        early(0, 2)
        ycopies = {}

        def over_links(p, a, t):
            p_ref = part.at[s, p]
            if p == 0 and a < 3:
                send(
                    block(p_ref, t * 4 + (y + 2) % 4), xbuf.at[s, zl],
                    rs_s.at[s, p, 15 + a], rs_r.at[s, p, 16 + zl], z_to[a],
                )
            for j, d in enumerate(shifts):
                if p == 0 and j == 0:
                    continue
                n = a * 3 + j
                ycopies[p, a, j] = send(
                    block(p_ref, t * 4 + (y + d) % 4), ybuf.at[s, p, n],
                    rs_s.at[s, p, n], rs_r.at[s, p, n], y_to[j],
                )

        for p in range(PARTS):
            if p > 0:
                early(p, 1)
                early(p, 2)
            copies[p, 5].wait_recv()
            copies[p, 12].wait_recv()

            p_ref = part.at[s, p]
            cols = pl.ds(pl.multiple_of(x_from[0] * GROUP, 128), GROUP)
            right = gath[s, p, rows(x_from[0] * GROUP, GROUP), :]
            for a, t in enumerate(z_other + [zl]):
                at = rows(t * GROUP, GROUP)
                total = acc[p, at, :] + dot(cinv[at, cols], right)
                acc[p, at, :] = total
                p_ref[at, :] = total.astype(BF16)
                if a < 3:
                    over_links(p, a, t)
        for p in range(PARTS):
            over_links(p, 3, zl)
        after()

        def over_y(p, a, t):
            ways = (1, 2) if p == 0 else (0, 1, 2)
            for j in ways:
                ycopies[p, a, j].wait_recv()
            total = acc[p, rows((t * 4 + y) * CPD, CPD), :]
            for j in ways:
                total = total + ybuf[s, p, a * 3 + j].astype(F32)
            return total

        def toward_owner(p, a):
            qbuf[s, p, a] = over_y(p, a, z_other[a]).astype(BF16)
            send(
                qbuf.at[s, p, a], zbuf.at[s, p, zl],
                rs_s.at[s, p, 12 + a], rs_r.at[s, p, 12 + zl], z_to[a],
            )

        def arrived(p, a, src, dst, at):
            t = z_other[a]
            pltpu.make_async_remote_copy(
                src_ref=src.at[a], dst_ref=dst.at[t],
                send_sem=rs_s.at[s, p, 12 + a], recv_sem=rs_r.at[s, p, at + t],
                device_id=z_to[a], device_id_type=MESH,
            ).wait_recv()
            return dst[t].astype(F32)

        for a in range(3):
            toward_owner(0, a)
        toward_owner(1, 0)
        total = acc[0, rows((zl * 4 + (y + 2) % 4) * CPD, CPD), :]
        for a in range(3):
            total = total + arrived(0, a, qbuf.at[s, 0], xbuf.at[s], 16)
        xsum[s] = total.astype(BF16)
        from_far = send(xsum.at[s], xin.at[s], rs_s.at[s, 0, 18], rs_r.at[s, 0, 20], y_to[0])
        for a in (1, 2):
            toward_owner(1, a)
        for p in range(PARTS):
            total = over_y(p, 3, zl)
            for a in (2, 1, 0):
                total = total + arrived(p, a, qbuf.at[s, p], zbuf.at[s, p], 12)
            if p == 0:
                from_far.wait_recv()
                total = total + xin[s].astype(F32)
            coarse_b[:, lanes(p)] = total.astype(BF16)
            moved = dot(sbt[...], coarse_b[:, lanes(p)])
            if s > 0:
                moved = moved + face[:, lanes(p)]
            face[:, lanes(p)] = moved
            face_b[2 * s, p] = moved.astype(BF16)
            halo_start(2 * s, p)

    def prepare_faces():
        for i in (2, 3):
            loads[i].wait()
        w = [couple[0, f : f + 1, :] for f in range(4)]
        for m in range(4):
            at = pl.ds(m * 256, 256)
            ids = lax.broadcasted_iota(jnp.int32, (256, OVL), 0) + m * 256
            total = jnp.zeros((256, OVL), F32)
            for f in range(4):
                hit = ids == margin[0, f : f + 1, :]
                st[at, pl.ds(f * OVL, OVL)] = jnp.where(hit, 1.0, 0.0).astype(BF16)
                total = total + jnp.where(hit, w[f], 0.0)
            wrow[at, :] = jnp.broadcast_to(jnp.sum(total, axis=1, keepdims=True), (256, OVL))
        keep(4, st, st_out)
        keep(5, wrow, wrow_out)
        loads[5].wait()

    def prepare_local():
        loads[4].wait()
        wide = jnp.concatenate([couple[0, f : f + 1, :] for f in range(4)], axis=1)
        picked = dot(basis[...], st[...])
        bs[...] = (picked * wide).astype(BF16)
        sbt[...] = picked.T.astype(BF16)
        bt[...] = basis[...].astype(F32).T.astype(BF16)
        for m in range(4):
            at = pl.ds(m * 256, 256)
            lsw[at, :] = (dot(linv[at, :], st[...]) * wide).astype(BF16)
        for m in range(4):
            pick = st[:, m * OVL : (m + 1) * OVL].astype(F32).T.astype(BF16)
            at = pl.ds(m * OVL, OVL)
            sl[at, :] = dot(pick, linv[...]).astype(BF16)
            slsw[at, :] = dot(pick, lsw[...]).astype(BF16)

    def tiles(fn, size=256, total=NLOC):
        for m in range(total // size):
            fn(pl.ds(m * size, size))

    kept = []

    def keep(n, src, dst):
        cp = pltpu.make_async_copy(src, dst, out_sem.at[n])
        cp.start()
        kept.append(cp)

    loads[0].wait()
    base_b[...] = rhs[...].astype(BF16)
    loads[1].wait()
    first = dot(basis[...], base_b[...]).astype(BF16)
    for p in range(PARTS):
        gath[0, p, rows(c * CPD, CPD), :] = first[:, p * WIDTH : (p + 1) * WIDTH]
    for cp in loads[4:]:
        cp.start()
    pl.semaphore_wait(barrier, count)
    for p in range(PARTS):
        gather_z(0, p)
    for p in range(PARTS):
        gather_rest(0, p)

    for s in range(STEPS):
        h = 2 * s
        last = s == STEPS - 1
        coarse(s, *((prepare_faces, prepare_local) if s == 0 else (lambda: None,) * 2))

        def correct(at):
            v = dot(bt[at, :], coarse_b[...])
            if s > 0:
                v = v + sol[at, :]
            sol[at, :] = v
            vb[at, :] = v.astype(BF16)

        tiles(correct)
        if s == 0:
            loads[6].wait()

        def defect(at):
            base_b[at, :] = (rhs[at, :] - dot(lmat[at, :], vb[...])).astype(BF16)

        tiles(defect)

        def face_pre(at):
            pre_face[at, :] = face[at, :] + dot(sl[at, :], base_b[...])

        tiles(face_pre, 256, FACES)

        for p in range(PARTS):
            halo_wait(h, p)
            moved = pre_face[:, lanes(p)] + dot(slsw[...], recv[h, p])
            face[:, lanes(p)] = moved
            face_b[h + 1, p] = moved.astype(BF16)
            halo_start(h + 1, p)

        def solve(at):
            v = sol[at, :] + dot(linv[at, :], base_b[...])
            for p in range(PARTS):
                w = v[:, p * WIDTH : (p + 1) * WIDTH] + dot(lsw[at, :], recv[h, p])
                sol[at, lanes(p)] = w
                vb[at, lanes(p)] = w.astype(BF16)

        tiles(solve)
        if last:
            keep(0, sol, sol_out)

        def defect2(at):
            v = rhs[at, :] - dot(lmat[at, :], vb[...])
            if last:
                base[at, :] = v
            else:
                base_b[at, :] = v.astype(BF16)

        tiles(defect2)
        if not last:
            pre[...] = dot(basis[...], base_b[...])
            for p in range(PARTS):
                halo_wait(h + 1, p)
                gath[s + 1, p, rows(c * CPD, CPD), :] = (
                    pre[:, lanes(p)] + dot(bs[...], recv[h + 1, p])
                ).astype(BF16)
                gather_z(s + 1, p)
                gather_rest(s + 1, p)
        else:
            keep(1, base, base_out)
            for p in range(PARTS):
                halo_wait(h + 1, p)
                keep(2 + p, recv.at[h + 1, p], recv_out.at[p])

    for cp in kept:
        cp.wait()
    for cp in sends:
        cp.wait_send()
    halo_sent()


def last_residual(sol, base, recv, st, wrow, sol_out, res_out, res, sem):
    copies = [pltpu.make_async_copy(sol, sol_out, sem.at[4])]
    copies[0].start()
    right = jnp.concatenate([recv[p] for p in range(PARTS)], axis=1)
    for m in range(4):
        at = pl.ds(m * 256, 256)
        w = jnp.concatenate([wrow[at, :]] * PARTS, axis=1)
        res[at, :] = base[at, :] + w * dot(st[at, :], right)
        cp = pltpu.make_async_copy(res.at[at], res_out.at[at], sem.at[m])
        cp.start()
        copies.append(cp)
    for cp in copies:
        cp.wait()


def per_device(*args):
    args = [pltpu.with_memory_space_constraint(a, pltpu.HBM) for a in args]
    any_space = pl.BlockSpec(memory_space=pl.ANY)
    vm = pltpu.VMEM
    dma = pltpu.SemaphoreType.DMA
    scratch = [vm(a.shape, a.dtype) for a in args] + [
        vm((NLOC, NRHS), F32),
        vm((NLOC, NRHS), F32),
        vm((NLOC, NRHS), BF16),
        vm((NLOC, NRHS), BF16),
        vm((FACES, NRHS), F32),
        vm((2 * STEPS, PARTS, FACES, WIDTH), BF16),
        vm((2 * STEPS, PARTS, FACES, WIDTH), BF16),
        vm((STEPS, PARTS, COARSE_BLOCK, WIDTH), BF16),
        vm((PARTS, COARSE_BLOCK, WIDTH), F32),
        vm((STEPS, PARTS, COARSE_BLOCK, WIDTH), BF16),
        vm((STEPS, PARTS, 12, CPD, WIDTH), BF16),
        vm((STEPS, PARTS, 3, CPD, WIDTH), BF16),
        vm((STEPS, PARTS, 4, CPD, WIDTH), BF16),
        vm((STEPS, 4, CPD, WIDTH), BF16),
        vm((STEPS, CPD, WIDTH), BF16),
        vm((STEPS, CPD, WIDTH), BF16),
        vm((NLOC, FACES), BF16),
        vm((NLOC, OVL), F32),
        vm((CPD, FACES), BF16),
        vm((FACES, CPD), BF16),
        vm((NLOC, CPD), BF16),
        vm((NLOC, FACES), BF16),
        vm((FACES, NLOC), BF16),
        vm((FACES, FACES), BF16),
        vm((CPD, NRHS), F32),
        vm((FACES, NRHS), F32),
        vm((CPD, NRHS), BF16),
        dma((STEPS, PARTS, 15)), dma((STEPS, PARTS, 15)),
        dma((STEPS, PARTS, 19)), dma((STEPS, PARTS, 21)),
        dma((2 * STEPS, PARTS, 4)), dma((2 * STEPS, PARTS, 4)),
        dma((len(args),)), dma((6,)),
    ]
    out = jax.ShapeDtypeStruct((NLOC, NRHS), F32)
    handed_on = (
        out,
        out,
        jax.ShapeDtypeStruct((PARTS, FACES, WIDTH), BF16),
        jax.ShapeDtypeStruct((NLOC, FACES), BF16),
        jax.ShapeDtypeStruct((NLOC, OVL), F32),
    )
    handed = pl.pallas_call(
        kernel,
        out_shape=handed_on,
        in_specs=[any_space] * len(args),
        out_specs=(any_space,) * 5,
        scratch_shapes=scratch,
        name="schwarz",
        compiler_params=pltpu.CompilerParams(
            collective_id=0, has_side_effects=True, vmem_limit_bytes=48 << 20
        ),
    )(*args)
    return pl.pallas_call(
        last_residual,
        out_shape=(out, out),
        in_specs=[any_space] + [pl.BlockSpec(memory_space=vm)] * 4,
        out_specs=(pl.BlockSpec(memory_space=pltpu.HBM), pl.BlockSpec(memory_space=pltpu.HBM)),
        scratch_shapes=[vm((NLOC, NRHS), F32), dma((5,))],
        name="last_residual",
        compiler_params=pltpu.CompilerParams(vmem_limit_bytes=24 << 20),
    )(*handed)


def solution(mesh):
    whole = P(("row", "col"), None)
    stacked = P(("row", "col"), None, None)
    return jax.shard_map(
        per_device,
        mesh=mesh,
        in_specs=(whole, whole, whole, whole, P("col", "row"), stacked, stacked),
        out_specs=(whole, whole),
        check_vma=False,
    )
```
